512 devices in a mesh: seq: 32 (over z_lo, y, core), chan: 4 (over z_hi), dp: 4 (over x).
Axes of the slice: x: 4, y: 4, z: 16 (z_hi: 4, z_lo: 4; z = z_hi * 4 + z_lo), core: 2. Of those that a mesh axis runs over, the one named last changes fastest.
Arguments:
- inputs: bfloat16 [4, 65536, 1024], P('dp', 'seq', 'chan'), may hold values from -6 to 6
- w_value: bfloat16 [4, 256, 256], P('chan'), may hold values from -0.375 to 0.375
- w_gate: bfloat16 [4, 256, 256], P('chan'), may hold values from -0.375 to 0.375
- w_out: bfloat16 [4, 256, 256], P('chan'), may hold values from -0.375 to 0.375
- mon_right: bfloat16 [256, 256], replicated, may hold values from -0.375 to 0.375
- mon_left: bfloat16 [256, 256], replicated, may hold values from -0.375 to 0.375
- twiddle: float32 [256, 256], P('seq'), may hold values from 0.4 to 1.6
- cotangent: bfloat16 [4, 65536, 1024], P('dp', 'seq', 'chan'), may hold values from -6 to 6
Outputs:
- grad_inputs: bfloat16 [4, 65536, 1024], P('dp', 'seq', 'chan')
- grad_value: float32 [4, 256, 256], P('chan')
- grad_gate: float32 [4, 256, 256], P('chan')
- grad_out: float32 [4, 256, 256], P('chan')
- grad_right: float32 [256, 256], replicated
- grad_left: float32 [256, 256], replicated
- grad_twiddle: float32 [256, 256], P('seq')
The draws below stay inside these ranges and needn't reach their ends.
All inputs are finite; a program needn't handle non-finite values.
Results may differ from the reference program's by a relative error of at most 0.015.
Values may be sent and summed in bfloat16 or wider, within the bound.
No kernel may reach another device: no remote copies, remote signals or barrier semaphores. Data moves between devices by JAX's collectives and lax.ppermute only.
A program may use at most 64 MiB of HBM per device.

```python
import jax
import jax.numpy as jnp
from jax import lax

CB = 256
BS = 256
NB = 256
SEQS = 4
L = 65536
NCB = 4
C = 1024


def block_scale(key, shape, split, smallest, top_value):
    factor_of = 1.0
    for dim, blocks in split:
        heights = jax.random.uniform(jax.random.fold_in(jax.random.fold_in(key, 6), dim), (blocks,), jnp.float32, smallest / len(split), top_value / len(split))
        factor_of = factor_of * jnp.repeat(jnp.exp(heights), shape[dim] // blocks).reshape((-1,) + (1,) * (len(shape) - 1 - dim))
    return factor_of


def scatter_about(own_key, dims, scale, limit, shards=(), dtype=jnp.bfloat16):
    result = scale * jax.random.normal(own_key, dims, jnp.float32)
    if shards:
        result = result * block_scale(own_key, dims, shards, -0.22, 0.18)
    return jnp.clip(result, -limit, limit).astype(dtype)


def setup_inputs(seed: int = 0) -> dict:
    key_list = jax.random.split(jax.random.key(seed), 9)
    return {
        "inputs": scatter_about(key_list[0], (SEQS, L, C), 1.0, 6.0, ((0, 4), (1, 32), (2, 4))),
        "w_value": scatter_about(key_list[1], (NCB, CB, CB), CB ** -0.5, 0.375, ((0, 4),)),
        "w_gate": scatter_about(key_list[2], (NCB, CB, CB), CB ** -0.5, 0.375, ((0, 4),)),
        "w_out": scatter_about(key_list[3], (NCB, CB, CB), CB ** -0.5, 0.375, ((0, 4),)),
        "mon_right": scatter_about(key_list[4], (BS, BS), BS ** -0.5, 0.375),
        "mon_left": scatter_about(key_list[5], (NB, NB), NB ** -0.5, 0.375),
        "twiddle": jnp.clip(0.4 + 1.2 * jax.random.uniform(key_list[6], (NB, BS), jnp.float32) ** block_scale(key_list[6], (NB, BS), ((0, 32),), -0.2, 0.2), 0.4, 1.6),
        "cotangent": scatter_about(key_list[7], (SEQS, L, C), 1.0, 6.0, ((0, 4), (1, 32), (2, 4))),
    }


def block_mix(input_activations, weights):
    parts = input_activations.reshape(NB * BS, NCB, CB).astype(jnp.float32)
    out = jnp.einsum('lbc,bcd->lbd', parts, weights.astype(jnp.float32))
    return out.reshape(NB * BS, NCB * CB)

def block_back(input_activations, weights):
    parts = input_activations.reshape(NB * BS, NCB, CB).astype(jnp.float32)
    out = jnp.einsum('lbd,bcd->lbc', parts, weights.astype(jnp.float32))
    return out.reshape(NB * BS, NCB * CB)

def block_grad(left, right):
    first = left.reshape(NB * BS, NCB, CB).astype(jnp.float32)
    second = right.reshape(NB * BS, NCB, CB).astype(jnp.float32)
    return jnp.einsum('lbc,lbd->bcd', first, second)

def reference(inputs, w_value, w_gate, w_out, mon_right, mon_left, twiddle, cotangent):
    right32 = mon_right.astype(jnp.float32)
    left32 = mon_left.astype(jnp.float32)

    def one_sequence(pair):
        input_activations, upstream = pair
        values = block_mix(input_activations, w_value).astype(jnp.bfloat16)
        gates = block_mix(input_activations, w_gate).astype(jnp.bfloat16)
        cube = values.reshape(NB, BS, NCB * CB).astype(jnp.float32)
        rotated = jnp.einsum('jk,ikc->ijc', right32, cube)
        twisted = (rotated * twiddle[:, :, None]).astype(jnp.bfloat16)
        mixed = jnp.einsum('ik,kjc->ijc', left32, twisted.astype(jnp.float32)).astype(jnp.bfloat16)
        mixed = mixed.reshape(NB * BS, NCB * CB)
        gated_values = (gates.astype(jnp.float32) * mixed.astype(jnp.float32)).astype(jnp.bfloat16)
        g_out = block_grad(gated_values, upstream)
        back_gated = block_back(upstream, w_out).astype(jnp.bfloat16)
        back_mixed = (back_gated.astype(jnp.float32) * gates.astype(jnp.float32)).astype(jnp.bfloat16)
        gate_cotangents = (back_gated.astype(jnp.float32) * mixed.astype(jnp.float32)).astype(jnp.bfloat16)
        back_cube = back_mixed.reshape(NB, BS, NCB * CB).astype(jnp.float32)
        back_twisted = jnp.einsum('ik,ijc->kjc', left32, back_cube).astype(jnp.bfloat16)
        g_left = jnp.einsum('ijc,kjc->ik', back_cube, twisted.astype(jnp.float32))
        g_twiddle = lax.optimization_barrier(jnp.sum(back_twisted.astype(jnp.float32) * rotated, axis=2))
        back_rotated = (back_twisted.astype(jnp.float32) * twiddle[:, :, None]).astype(jnp.bfloat16)
        value_cotangents = jnp.einsum('jk,ijc->ikc', right32, back_rotated.astype(jnp.float32)).astype(jnp.bfloat16)
        g_right = jnp.einsum('ijc,ikc->jk', back_rotated.astype(jnp.float32), cube)
        value_cotangents = value_cotangents.reshape(NB * BS, NCB * CB)
        grad_acts = (block_back(value_cotangents, w_value) + block_back(gate_cotangents, w_gate)).astype(jnp.bfloat16)
        g_value = block_grad(input_activations, value_cotangents)
        g_gate = block_grad(input_activations, gate_cotangents)
        return (grad_acts, (g_value, g_gate, g_out, g_right, g_left, g_twiddle))
    grad_inputs, stacked = lax.map(one_sequence, (inputs, cotangent))
    g_value, g_gate, g_out, g_right, g_left, g_twiddle = [lax.optimization_barrier(jnp.sum(item, axis=0)) for item in stacked]
    return (grad_inputs, g_value, g_gate, g_out, g_right, g_left, g_twiddle)
```

```python
import jax
import jax.numpy as jnp
from jax import lax
from jax.sharding import PartitionSpec as P

F32 = jnp.float32
BF16 = jnp.bfloat16


def channel_product(rows, weight):
    return jnp.einsum("nfj,jr->nfr", rows, weight, preferred_element_type=F32)


def channel_back(rows, weight):
    return jnp.einsum("bxj,rj->bxr", rows, weight, preferred_element_type=F32)


def across_blocks(left_factor, columns):
    return jnp.einsum(
        "ik,skjc->sijc", left_factor, columns, preferred_element_type=F32
    ).astype(BF16)


def across_back(left_factor, columns):
    return jnp.einsum(
        "ik,sijc->skjc", left_factor, columns, preferred_element_type=F32
    ).astype(BF16)


def swap(array, axis, size, step):
    return lax.ppermute(array, axis, [(i, i ^ step) for i in range(size)])


def scatter_sum(parts, axis):
    size = parts.shape[0]
    me = lax.axis_index(axis)
    total = lax.dynamic_index_in_dim(parts, me, 0, keepdims=False).astype(F32)
    for step in range(1, size):
        out = lax.dynamic_index_in_dim(parts, me ^ step, 0, keepdims=False)
        total = total + swap(out, axis, size, step).astype(F32)
    return total


def exchange_sum(array, axis, size):
    one, two, three = (swap(array, axis, size, step) for step in (1, 2, 3))
    return (array + one) + (two + three)


def gather(array, axis, size):
    me = lax.axis_index(axis)
    out = jnp.zeros((size,) + array.shape, array.dtype)
    for step in range(size):
        part = array if step == 0 else swap(array, axis, size, step)
        out = lax.dynamic_update_index_in_dim(out, part, me ^ step, 0)
    return out


def on_device(sizes, inputs, w_value, w_gate, w_out, mon_right, mon_left, twiddle, cotangent):
    seq_size, chan_size, dp_size = sizes
    seq_count, local_len, width = inputs.shape
    block_size = mon_right.shape[0]
    local_blocks = local_len // block_size
    value_weight = w_value[0]
    gate_weight = w_gate[0]
    out_weight = w_out[0]
    gates = channel_product(inputs, gate_weight).astype(BF16)
    back_gated = channel_back(cotangent, out_weight).astype(BF16)
    back_mixed = (back_gated.astype(F32) * gates.astype(F32)).astype(BF16)
    back_cube = back_mixed.reshape(seq_count, local_blocks, block_size, width)
    back_cols = lax.all_to_all(back_cube, "seq", split_axis=2, concat_axis=1, tiled=True)
    values = channel_product(inputs, value_weight).astype(BF16)
    cube = values.reshape(seq_count, local_blocks, block_size, width)
    rotated = jnp.einsum("jk,sikc->sijc", mon_right, cube, preferred_element_type=F32)
    twist_rows = twiddle[None, :, :, None]
    twisted = (rotated * twist_rows).astype(BF16)
    twist_cols = lax.all_to_all(twisted, "seq", split_axis=2, concat_axis=1, tiled=True)
    back_twist_cols = across_back(mon_left, back_cols)
    back_twisted = lax.all_to_all(back_twist_cols, "seq", split_axis=1, concat_axis=2, tiled=True)
    mixed_cols = across_blocks(mon_left, twist_cols)
    mixed_cube = lax.all_to_all(mixed_cols, "seq", split_axis=1, concat_axis=2, tiled=True)
    left_part = jnp.einsum("sijc,skjc->ik", back_cols, twist_cols, preferred_element_type=F32)
    back_twist32 = back_twisted.astype(F32)
    twiddle_part = jnp.sum(back_twist32 * rotated, axis=(0, 3))
    back_rotated = (back_twist32 * twist_rows).astype(BF16)
    value_cotangents = jnp.einsum(
        "jk,sijc->sikc", mon_right, back_rotated, preferred_element_type=F32
    ).astype(BF16)
    right_part = jnp.einsum("sijc,sikc->jk", back_rotated, cube, preferred_element_type=F32)
    value_cotangents = value_cotangents.reshape(seq_count, local_len, width)
    value_part = jnp.einsum("yrz,yrj->zj", inputs, value_cotangents, preferred_element_type=F32)
    mixed = mixed_cube.reshape(seq_count, local_len, width)
    gated = (gates.astype(F32) * mixed.astype(F32)).astype(BF16)
    out_part = jnp.einsum("yrz,yrj->zj", gated, cotangent, preferred_element_type=F32)
    gate_cotangents = (back_gated.astype(F32) * mixed.astype(F32)).astype(BF16)
    gate_part = jnp.einsum("yrz,yrj->zj", inputs, gate_cotangents, preferred_element_type=F32)
    grad_inputs = (
        channel_back(value_cotangents, value_weight) + channel_back(gate_cotangents, gate_weight)
    ).astype(BF16)

    lanes = 128
    five = jnp.stack([value_part, gate_part, out_part, right_part, left_part])
    five = five.reshape(5, dp_size, -1, lanes).swapaxes(0, 1)
    five_rows = five.shape[2]
    twist = twiddle_part.reshape(dp_size, -1, lanes)
    twist_len = twist.shape[1]
    packed = jnp.concatenate(
        [five.reshape(dp_size, 5 * five_rows, lanes), twist], axis=1
    ).astype(BF16)
    mine = scatter_sum(packed, "dp")
    five_mine = mine[: 5 * five_rows].reshape(5, seq_size, -1, lanes).swapaxes(0, 1)
    piece = five_mine.shape[2]
    arrived = lax.all_to_all(five_mine.astype(BF16), "seq", split_axis=0, concat_axis=0, tiled=True)
    summed = jnp.sum(arrived.astype(F32), axis=0)
    tail = jnp.concatenate(
        [summed[3:].reshape(2 * piece, lanes), mine[5 * five_rows :]], axis=0
    )
    tail = exchange_sum(tail, "chan", chan_size)
    twist_sum = tail[2 * piece :].astype(BF16)
    done = jnp.concatenate([summed[:3], tail[: 2 * piece].reshape(2, piece, lanes)]).astype(BF16)
    spread = jnp.broadcast_to(done[None], (seq_size,) + done.shape)
    whole = lax.all_to_all(spread, "seq", split_axis=0, concat_axis=0, tiled=True)
    whole = whole.swapaxes(0, 1).reshape(5 * five_rows, lanes)
    final = gather(jnp.concatenate([whole, twist_sum], axis=0), "dp", dp_size).astype(F32)
    grads = final[:, : 5 * five_rows].reshape(dp_size, 5, five_rows, lanes).swapaxes(0, 1)
    grads = grads.reshape(5, width, -1)
    twiddle_sum = final[:, 5 * five_rows :].reshape(twiddle.shape)
    return (
        grad_inputs,
        grads[0][None],
        grads[1][None],
        grads[2][None],
        grads[3],
        grads[4],
        twiddle_sum,
    )


def solution(mesh):
    sizes = tuple(mesh.shape[name] for name in ("seq", "chan", "dp"))

    def body(*args):
        return on_device(sizes, *args)

    return jax.shard_map(
        body,
        mesh=mesh,
        in_specs=(
            P("dp", "seq", "chan"),
            P("chan", None, None),
            P("chan", None, None),
            P("chan", None, None),
            P(),
            P(),
            P("seq", None),
            P("dp", "seq", "chan"),
        ),
        out_specs=(
            P("dp", "seq", "chan"),
            P("chan", None, None),
            P("chan", None, None),
            P("chan", None, None),
            P(),
            P(),
            P("seq", None),
        ),
        check_vma=False,
    )
```

```python
import functools

import jax
import jax.numpy as jnp
from jax import lax
from jax.experimental import pallas as pl
from jax.experimental.pallas import tpu as pltpu
from jax.sharding import PartitionSpec as P

F32 = jnp.float32
BF16 = jnp.bfloat16
LANES = 128
VMEM = pl.BlockSpec(memory_space=pltpu.VMEM)
PARAMS = pltpu.CompilerParams(vmem_limit_bytes=50 * 1024 * 1024)


def dot(a, b, dims=((1,), (0,))):
    return lax.dot_general(a, b, (dims, ((), ())), preferred_element_type=F32)


NT = ((1,), (1,))
TN = ((0,), (0,))


def put_wide(ref, value):
    for h in range(ref.shape[0]):
        ref[h] = value[:, h * LANES : (h + 1) * LANES]


def get_wide(ref):
    return jnp.concatenate([ref[h] for h in range(ref.shape[0])], axis=1)


def every(ref, start, count, step, halves=range(2)):
    return jnp.concatenate([ref[h, pl.ds(start, count, stride=step), :] for h in halves], axis=1)


def put_every(ref, start, count, step, value, first=0):
    for h in range(value.shape[1] // LANES):
        ref[first + h, pl.ds(start, count, stride=step), :] = value[:, h * LANES : (h + 1) * LANES]


def place_major(ref, groups, places, halves=range(2)):
    return jnp.concatenate([every(ref, p, groups, places, halves) for p in range(places)], axis=0)


def place_major_tables(right_ref, twiddle_ref, wide, groups, places):
    put_wide(wide, right_ref[...].astype(F32))
    right = place_major(wide, groups, places).astype(BF16)
    rows = twiddle_ref.shape[0]
    wide[0] = jnp.concatenate(
        [twiddle_ref[...], jnp.zeros((LANES - rows, twiddle_ref.shape[1]), F32)], axis=0
    ).T
    twist = place_major(wide, groups, places, range(1))
    return right, twist


def rows_before(
    groups, x_ref, ct_ref, wv_ref, wg_ref, wo_ref, right_ref, twiddle_ref,
    send_ref, value_ref, gate_ref, back_ref, wide, cols,
):
    blocks = twiddle_ref.shape[0]
    size = right_ref.shape[0]
    places = size // groups
    right, twist = place_major_tables(right_ref, twiddle_ref, wide, groups, places)
    for i in range(blocks):
        rows = slice(i * size, (i + 1) * size)
        x = x_ref[rows, :]
        gates = dot(x, wg_ref[...]).astype(BF16)
        back = dot(ct_ref[rows, :], wo_ref[...], NT).astype(BF16)
        values = dot(x, wv_ref[...]).astype(BF16)
        gate_ref[rows, :] = gates
        back_ref[rows, :] = back
        value_ref[rows, :] = values
        put_wide(wide, back.astype(F32) * gates.astype(F32))
        twisted = dot(right, values) * twist[:, i : i + 1]
        for p in range(places):
            put_every(cols, i, groups, blocks, every(wide, p, groups, places), 2 * p)
            part = twisted[p * groups : (p + 1) * groups]
            put_every(cols, i, groups, blocks, part, 2 * (places + p))
    for t in range(4 * places):
        send_ref[:, t * LANES : (t + 1) * LANES] = cols[t].astype(BF16)


def columns(left_ref, cols_ref, send_ref, grad_ref):
    left = left_ref[...]
    half = cols_ref.shape[1] // 2
    step = 512
    for at in range(0, half, step):
        back = cols_ref[:, at : at + step]
        twist = cols_ref[:, half + at : half + at + step]
        send_ref[:, at : at + step] = dot(left, back, TN).astype(BF16)
        send_ref[:, half + at : half + at + step] = dot(left, twist).astype(BF16)
    grad_ref[...] = dot(cols_ref[:, :half], cols_ref[:, half:], NT)


def rows_after(
    groups, came_ref, x_ref, ct_ref, value_ref, gate_ref, back_ref, wv_ref, wg_ref,
    right_ref, twiddle_ref, left_grad_ref,
    gi_ref, low_ref, high_ref,
    wide, cols, gated_all, back_gates_all, back_values_all,
):
    blocks = twiddle_ref.shape[0]
    size = right_ref.shape[0]
    places = size // groups
    right, twist = place_major_tables(right_ref, twiddle_ref, wide, groups, places)
    for t in range(4 * places):
        cols[t] = came_ref[:, t * LANES : (t + 1) * LANES].astype(F32)
    lane = lax.broadcasted_iota(jnp.int32, (size, LANES), 1)
    right_grad = jnp.zeros((size, size), F32)
    twist_grad = jnp.zeros((size, LANES), F32)
    for i in range(blocks):
        rows = slice(i * size, (i + 1) * size)
        values = value_ref[rows, :]
        back = jnp.concatenate(
            [
                every(cols, i, groups, blocks, (2 * p, 2 * p + 1))
                for p in range(places)
            ],
            axis=0,
        )
        rotated = dot(right, values)
        column = jnp.sum(back * rotated, axis=1, keepdims=True)
        twist_grad = jnp.where(lane == i, column, twist_grad)
        back_rotated = (back * twist[:, i : i + 1]).astype(BF16)
        back_values = dot(right, back_rotated, TN).astype(BF16)
        right_grad += dot(back_rotated, values, NT)
        for p in range(places):
            at = 2 * (places + p)
            put_every(wide, p, groups, places, every(cols, i, groups, blocks, (at, at + 1)))
        mixed = get_wide(wide)
        back_gates = (back_ref[rows, :].astype(F32) * mixed).astype(BF16)
        gated_all[rows, :] = (gate_ref[rows, :].astype(F32) * mixed).astype(BF16)
        back_gates_all[rows, :] = back_gates
        back_values_all[rows, :] = back_values
        gi_ref[rows, :] = (
            dot(back_values, wv_ref[...], NT) + dot(back_gates, wg_ref[...], NT)
        ).astype(BF16)

    def put(ref, tile, grad):
        for h in range(2):
            ref[h * size : (h + 1) * size, tile * LANES : (tile + 1) * LANES] = grad[
                :, h * LANES : (h + 1) * LANES
            ].astype(BF16)

    put(low_ref, 0, dot(x_ref[...], back_values_all[...], TN))
    put(high_ref, 0, dot(x_ref[...], back_gates_all[...], TN))
    put(low_ref, 1, dot(gated_all[...], ct_ref[...], TN))
    put(high_ref, 2, left_grad_ref[...])
    for p in range(places):
        put_every(wide, p, groups, places, right_grad[p * groups : (p + 1) * groups])
    put(low_ref, 2, get_wide(wide))
    for p in range(places):
        put_every(wide, p, groups, places, twist_grad[p * groups : (p + 1) * groups])
    flat = wide[0].T[:blocks]
    own = jnp.concatenate([flat[:, :LANES], flat[:, LANES:]], axis=0).astype(BF16)
    high_ref[:, LANES : 2 * LANES] = jnp.zeros((2 * size, LANES), BF16)
    at = pl.multiple_of(lax.axis_index("seq") * 2 * blocks, 2 * blocks)
    high_ref[pl.ds(at, 2 * blocks), LANES : 2 * LANES] = own


def unpack(mine_ref, other_ref, value_ref, gate_ref, out_ref, right_ref, left_ref, twiddle_ref):
    size = value_ref.shape[0]
    blocks = twiddle_ref.shape[0]
    seq = lax.axis_index("seq")

    def take(ref, source, tile):
        for h in range(2):
            ref[:, h * LANES : (h + 1) * LANES] = source[
                h * size : (h + 1) * size, tile * LANES : (tile + 1) * LANES
            ].astype(F32)

    def spread(low, high):
        take(value_ref, low, 0)
        take(out_ref, low, 1)
        take(right_ref, low, 2)
        take(gate_ref, high, 0)
        take(left_ref, high, 2)
        at = pl.multiple_of(seq * 2 * blocks, 2 * blocks)
        own = high[pl.ds(at, 2 * blocks), LANES : 2 * LANES].astype(F32)
        twiddle_ref[:, :LANES] = own[:blocks]
        twiddle_ref[:, LANES:] = own[blocks:]

    @pl.when(seq % 2 == 0)
    def _():
        spread(mine_ref, other_ref)

    @pl.when(seq % 2 == 1)
    def _():
        spread(other_ref, mine_ref)


def shape(*dims, dtype=BF16):
    return jax.ShapeDtypeStruct(dims, dtype)


def cost(flops, moved):
    return pl.CostEstimate(flops=int(flops), bytes_accessed=int(moved), transcendentals=0)


def on_device(sizes, inputs, w_value, w_gate, w_out, mon_right, mon_left, twiddle, cotangent):
    seq_size, chan_size, dp_size = sizes
    _, length, width = inputs.shape
    size = mon_right.shape[0]
    blocks = length // size
    places = size // seq_size
    x, ct = inputs[0], cotangent[0]
    cols = places * width
    square = 2 * length * width * width

    send, values, gates, back_gated = pl.pallas_call(
        functools.partial(rows_before, seq_size),
        out_shape=(shape(seq_size * blocks, 2 * cols),) + (shape(length, width),) * 3,
        in_specs=[VMEM] * 7,
        out_specs=(VMEM,) * 4,
        scratch_shapes=[
            pltpu.VMEM((2, size, LANES), F32),
            pltpu.VMEM((4 * places, seq_size * blocks, LANES), F32),
        ],
        compiler_params=PARAMS,
        cost_estimate=cost(4 * square, 14 * length * width),
        name="rows_before",
    )(x, ct, w_value[0], w_gate[0], w_out[0], mon_right, twiddle)
    came = lax.all_to_all(send, "seq", 0, 0, tiled=True)
    send_back, left_grad = pl.pallas_call(
        columns,
        out_shape=(shape(seq_size * blocks, 2 * cols), shape(size, size, dtype=F32)),
        in_specs=[VMEM] * 2,
        out_specs=(VMEM,) * 2,
        compiler_params=PARAMS,
        cost_estimate=cost(3 * square, 8 * length * width),
        name="columns",
    )(mon_left, came)
    came_back = lax.all_to_all(send_back, "seq", 0, 0, tiled=True)
    grad_inputs, low, high = pl.pallas_call(
        functools.partial(rows_after, seq_size),
        out_shape=(
            shape(length, width),
            shape(2 * size, 3 * LANES),
            shape(2 * size, 3 * LANES),
        ),
        in_specs=[VMEM] * 11,
        out_specs=(VMEM,) * 3,
        scratch_shapes=[
            pltpu.VMEM((2, size, LANES), F32),
            pltpu.VMEM((4 * places, seq_size * blocks, LANES), F32),
            pltpu.VMEM((length, width), BF16),
            pltpu.VMEM((length, width), BF16),
            pltpu.VMEM((length, width), BF16),
        ],
        compiler_params=PARAMS,
        cost_estimate=cost(8 * square, 16 * length * width),
        name="rows_after",
    )(
        came_back, x, ct, values, gates, back_gated,
        w_value[0], w_gate[0], mon_right, twiddle, left_grad,
    )

    even = lax.axis_index("seq") % 2 == 0
    swap = [(i, i ^ 1) for i in range(seq_size)]
    like = [
        [seq * dp_size + dp for seq in range(core, seq_size, 2) for dp in range(dp_size)]
        for core in range(2)
    ]
    peers = len(like[0])
    theirs = lax.ppermute(jnp.where(even, high, low), "seq", swap)
    pair = (jnp.where(even, low, high).astype(F32) + theirs.astype(F32)).astype(BF16)
    arrived = lax.all_to_all(pair, ("seq", "dp"), 0, 0, tiled=True, axis_index_groups=like)
    mine = jnp.sum(arrived.reshape(peers, -1, 3 * LANES).astype(F32), axis=0)
    factors = jnp.broadcast_to(mine[None, :, LANES:], (chan_size,) + mine[:, LANES:].shape)
    factors = jnp.sum(lax.all_to_all(factors, "chan", 0, 0, tiled=True), axis=0)
    middle = jnp.where(even, mine[:, LANES : 2 * LANES], factors[:, :LANES])
    done = jnp.concatenate([mine[:, :LANES], middle, factors[:, LANES:]], axis=1).astype(BF16)
    spread = jnp.broadcast_to(done[None], (peers,) + done.shape).reshape(pair.shape)
    half = lax.all_to_all(spread, ("seq", "dp"), 0, 0, tiled=True, axis_index_groups=like)
    other = lax.ppermute(half, "seq", swap)
    g_value, g_gate, g_out, g_right, g_left, g_twiddle = pl.pallas_call(
        unpack,
        out_shape=(shape(size, size, dtype=F32),) * 5 + (shape(blocks, size, dtype=F32),),
        in_specs=[VMEM] * 2,
        out_specs=(VMEM,) * 6,
        compiler_params=PARAMS,
        name="unpack",
    )(half, other)
    return grad_inputs[None], g_value[None], g_gate[None], g_out[None], g_right, g_left, g_twiddle


def solution(mesh):
    sizes = tuple(mesh.shape[name] for name in ("seq", "chan", "dp"))
    return jax.shard_map(
        functools.partial(on_device, sizes),
        mesh=mesh,
        in_specs=(
            P("dp", "seq", "chan"),
            P("chan", None, None),
            P("chan", None, None),
            P("chan", None, None),
            P(),
            P(),
            P("seq", None),
            P("dp", "seq", "chan"),
        ),
        out_specs=(
            P("dp", "seq", "chan"),
            P("chan", None, None),
            P("chan", None, None),
            P("chan", None, None),
            P(),
            P(),
            P("seq", None),
        ),
        check_vma=False,
    )
```

```python
import functools

import jax
import jax.numpy as jnp
from jax import lax
from jax.experimental import pallas as pl
from jax.experimental.pallas import tpu as pltpu
from jax.sharding import PartitionSpec as P

F32 = jnp.float32
BF16 = jnp.bfloat16
LANES = 128
VMEM = pl.BlockSpec(memory_space=pltpu.VMEM)
HBM = pl.BlockSpec(memory_space=pl.ANY)


def params(mib):
    return pltpu.CompilerParams(vmem_limit_bytes=mib * 1024 * 1024)


def dot(a, b, dims=((1,), (0,))):
    return lax.dot_general(a, b, (dims, ((), ())), preferred_element_type=F32)


NT = ((1,), (1,))
TN = ((0,), (0,))


def every(ref, start, count, step):
    return ref[pl.ds(start, count, stride=step), :]


def place_major(ref, groups, places):
    return jnp.concatenate([every(ref, p, groups, places) for p in range(places)], axis=0)


def group_major(ref, value, groups, places):
    for p in range(places):
        ref[pl.ds(p, groups, stride=places), :] = value[p * groups : (p + 1) * groups]
    return ref[...]


def shuffle(outer, inner):
    size = outer * inner
    row = lax.broadcasted_iota(jnp.int32, (size, size), 0)
    column = lax.broadcasted_iota(jnp.int32, (size, size), 1)
    return jnp.where(column == (row % inner) * outer + row // inner, 1.0, 0.0).astype(BF16)


def rows_before(
    groups, x_hbm, ct_hbm, wv_hbm, wg_hbm, wo_hbm, right_hbm, twiddle_hbm,
    send_hbm,
    x_ref, ct_ref, wv_ref, wg_ref, wo_ref, right_ref, twiddle_ref,
    send_ref, wide, cols, small_sems, in_sems, send_sems,
):
    blocks = twiddle_ref.shape[0]
    size = right_ref.shape[0]
    places = size // groups
    width = x_ref.shape[1]
    parts = in_sems.shape[1]
    step = x_ref.shape[0] // parts
    small = [
        pltpu.make_async_copy(source, target, small_sems.at[n])
        for n, (source, target) in enumerate(
            (
                (wg_hbm, wg_ref), (wo_hbm, wo_ref), (wv_hbm, wv_ref),
                (right_hbm, right_ref), (twiddle_hbm, twiddle_ref),
            )
        )
    ]
    for copy in small:
        copy.start()
    copies = []
    for n in range(parts):
        rows = pl.ds(n * step, step)
        copies.append(
            (
                pltpu.make_async_copy(x_hbm.at[rows], x_ref.at[rows], in_sems.at[0, n]),
                pltpu.make_async_copy(ct_hbm.at[rows], ct_ref.at[rows], in_sems.at[1, n]),
            )
        )
        for copy in copies[-1]:
            copy.start()
    to_places = shuffle(places, groups)
    for copy in small:
        copy.wait()
    right = dot(to_places, right_ref[...]).astype(BF16)
    wide[...] = jnp.concatenate(
        [twiddle_ref[...], jnp.zeros((LANES - blocks, size), F32)], axis=0
    ).T
    twist = place_major(wide, groups, places)
    out = []
    for i in range(blocks):
        rows = slice(i * size, (i + 1) * size)
        if i * size % step == 0:
            for copy in copies[i * size // step]:
                copy.wait()
        x = x_ref[rows, :]
        gates = dot(x, wg_ref[...]).astype(BF16)
        back = dot(ct_ref[rows, :], wo_ref[...], NT).astype(BF16)
        values = dot(x, wv_ref[...]).astype(BF16)
        mixed = (back.astype(F32) * gates.astype(F32)).astype(BF16)
        mixed = dot(to_places, mixed).astype(BF16)
        twisted = (dot(right, values) * twist[:, i : i + 1]).astype(BF16)
        for p in range(places):
            part = slice(p * groups, (p + 1) * groups)
            here = slice(i * groups, (i + 1) * groups)
            cols[here, p * width : (p + 1) * width] = mixed[part]
            cols[here, (places + p) * width : (places + p + 1) * width] = twisted[part]
    to_send = shuffle(groups, blocks)
    lanes = cols.shape[1] // send_sems.shape[0]
    for n in range(send_sems.shape[0]):
        at = slice(n * lanes, (n + 1) * lanes)
        send_ref[:, at] = dot(to_send, cols[:, at]).astype(BF16)
        part = pl.ds(n * lanes, lanes)
        out.append(
            pltpu.make_async_copy(send_ref.at[:, part], send_hbm.at[:, part], send_sems.at[n])
        )
        out[-1].start()
    for copy in out:
        copy.wait()


def columns(left_ref, cols_ref, send_ref, grad_ref):
    left = left_ref[...]
    half = cols_ref.shape[1] // 2
    for at in range(0, half, 512):
        back = cols_ref[:, at : at + 512]
        twist = cols_ref[:, half + at : half + at + 512]
        send_ref[:, at : at + 512] = dot(left, back, TN).astype(BF16)
        send_ref[:, half + at : half + at + 512] = dot(left, twist).astype(BF16)
    grad_ref[...] = dot(cols_ref[:, :half], cols_ref[:, half:], NT)


def rows_after(
    groups, came_hbm, x_hbm, ct_hbm, wv_hbm, wg_hbm, wo_hbm, right_hbm, twiddle_hbm, left_grad_hbm,
    gi_hbm, keep_hbm, give_hbm,
    gi_ref, low_ref, high_ref, came_ref, x_ref, ct_ref,
    wv_ref, wg_ref, wo_ref, right_ref, twiddle_ref, left_grad_ref,
    wide, cols, gated_all, back_gates_all, back_values_all,
    came_sems, small_sems, in_sems, out_sems, half_sems,
):
    size = right_ref.shape[0]
    blocks = twiddle_ref.shape[0]
    places = size // groups
    width = x_ref.shape[1]
    small = [
        pltpu.make_async_copy(source, target, small_sems.at[n])
        for n, (source, target) in enumerate(
            (
                (right_hbm, right_ref), (twiddle_hbm, twiddle_ref), (wv_hbm, wv_ref),
                (wg_hbm, wg_ref), (wo_hbm, wo_ref), (left_grad_hbm, left_grad_ref),
            )
        )
    ]
    for copy in small[:2]:
        copy.start()
    parts = came_sems.shape[0]
    lanes = came_ref.shape[1] // parts
    came = []
    for n in range(parts):
        at = pl.ds(n * lanes, lanes)
        came.append(
            pltpu.make_async_copy(came_hbm.at[:, at], came_ref.at[:, at], came_sems.at[n])
        )
        came[-1].start()
    for copy in small[2:]:
        copy.start()
    pieces = in_sems.shape[1]
    step = x_ref.shape[0] // pieces
    local = []
    for n in range(pieces):
        at = pl.ds(n * step, step)
        local.append(
            (
                pltpu.make_async_copy(x_hbm.at[at], x_ref.at[at], in_sems.at[0, n]),
                pltpu.make_async_copy(ct_hbm.at[at], ct_ref.at[at], in_sems.at[1, n]),
            )
        )
        for copy in local[-1]:
            copy.start()
    to_blocks = shuffle(blocks, groups)
    to_groups = shuffle(groups, places)
    for copy in small[:2]:
        copy.wait()
    right = dot(shuffle(places, groups), right_ref[...]).astype(BF16)
    right_turned = right.T
    wide[...] = jnp.concatenate(
        [twiddle_ref[...], jnp.zeros((LANES - blocks, size), F32)], axis=0
    ).T
    twist = place_major(wide, groups, places)
    for n in range(parts):
        at = slice(n * lanes, (n + 1) * lanes)
        came[n].wait()
        cols[:, at] = dot(to_blocks, came_ref[:, at]).astype(BF16)
    for copy in small[2:]:
        copy.wait()
    lane = lax.broadcasted_iota(jnp.int32, (size, LANES), 1)
    twist_grad = jnp.zeros((size, LANES), F32)
    right_grad = jnp.zeros((size, size), F32)
    out = []
    for i in range(blocks):
        rows = slice(i * size, (i + 1) * size)
        here = slice(i * groups, (i + 1) * groups)
        n = i * size // step
        if i * size % step == 0:
            for copy in local[n]:
                copy.wait()
        x = x_ref[rows, :]
        values = dot(x, wv_ref[...]).astype(BF16)
        gates = dot(x, wg_ref[...]).astype(BF16)
        back_gated = dot(ct_ref[rows, :], wo_ref[...], NT).astype(BF16)
        back, mixed = (
            jnp.concatenate(
                [
                    cols[here, (first + p) * width : (first + p + 1) * width]
                    for p in range(places)
                ],
                axis=0,
            )
            for first in (0, places)
        )
        back = back.astype(F32)
        column = jnp.sum(back * dot(right, values), axis=1, keepdims=True)
        twist_grad = jnp.where(lane == i, column, twist_grad)
        back_rotated = (back * twist[:, i : i + 1]).astype(BF16)
        back_values = dot(right_turned, back_rotated).astype(BF16)
        right_grad += dot(back_rotated, values, NT)
        mixed = dot(to_groups, mixed)
        back_gates = (back_gated.astype(F32) * mixed).astype(BF16)
        gated_all[rows, :] = (gates.astype(F32) * mixed).astype(BF16)
        back_gates_all[rows, :] = back_gates
        back_values_all[rows, :] = back_values
        gi_ref[rows, :] = (
            dot(back_values, wv_ref[...], NT) + dot(back_gates, wg_ref[...], NT)
        ).astype(BF16)
        if (i + 1) * size % step == 0:
            at = pl.ds(n * step, step)
            out.append(pltpu.make_async_copy(gi_ref.at[at], gi_hbm.at[at], out_sems.at[n]))
            out[-1].start()

    def put(ref, tile, grad):
        for h in range(2):
            ref[h * size : (h + 1) * size, tile * LANES : (tile + 1) * LANES] = grad[
                :, h * LANES : (h + 1) * LANES
            ].astype(BF16)

    put(low_ref, 0, dot(x_ref[...], back_values_all[...], TN))
    put(high_ref, 0, dot(x_ref[...], back_gates_all[...], TN))
    put(low_ref, 1, dot(gated_all[...], ct_ref[...], TN))
    put(high_ref, 2, left_grad_ref[...])
    for h in range(2):
        half = group_major(wide, right_grad[:, h * LANES : (h + 1) * LANES], groups, places)
        low_ref[h * size : (h + 1) * size, 2 * LANES :] = half.astype(BF16)
    flat = group_major(wide, twist_grad, groups, places).T[:blocks]
    own = jnp.concatenate([flat[:, :LANES], flat[:, LANES:]], axis=0).astype(BF16)
    high_ref[:, LANES : 2 * LANES] = jnp.zeros((2 * size, LANES), BF16)
    at = pl.multiple_of(lax.axis_index("seq") * 2 * blocks, 2 * blocks)
    high_ref[pl.ds(at, 2 * blocks), LANES : 2 * LANES] = own

    def leave(keep, give):
        copies = (
            pltpu.make_async_copy(keep, keep_hbm, half_sems.at[0]),
            pltpu.make_async_copy(give, give_hbm, half_sems.at[1]),
        )
        for copy in copies:
            copy.start()
        for copy in copies:
            copy.wait()

    even = lax.axis_index("seq") % 2 == 0

    @pl.when(even)
    def _():
        leave(low_ref, high_ref)

    @pl.when(jnp.logical_not(even))
    def _():
        leave(high_ref, low_ref)

    for copy in out:
        copy.wait()


def unpack(mine_ref, other_ref, value_ref, gate_ref, out_ref, right_ref, left_ref, twiddle_ref):
    size = value_ref.shape[0]
    blocks = twiddle_ref.shape[0]
    seq = lax.axis_index("seq")

    def take(ref, source, tile):
        for h in range(2):
            ref[:, h * LANES : (h + 1) * LANES] = source[
                h * size : (h + 1) * size, tile * LANES : (tile + 1) * LANES
            ].astype(F32)

    def spread(low, high):
        take(value_ref, low, 0)
        take(out_ref, low, 1)
        take(right_ref, low, 2)
        take(gate_ref, high, 0)
        take(left_ref, high, 2)
        at = pl.multiple_of(seq * 2 * blocks, 2 * blocks)
        own = high[pl.ds(at, 2 * blocks), LANES : 2 * LANES].astype(F32)
        twiddle_ref[:, :LANES] = own[:blocks]
        twiddle_ref[:, LANES:] = own[blocks:]

    @pl.when(seq % 2 == 0)
    def _():
        spread(mine_ref, other_ref)

    @pl.when(seq % 2 == 1)
    def _():
        spread(other_ref, mine_ref)


def shape(*dims, dtype=BF16):
    return jax.ShapeDtypeStruct(dims, dtype)


def cost(flops, moved):
    return pl.CostEstimate(flops=int(flops), bytes_accessed=int(moved), transcendentals=0)


def on_device(sizes, inputs, w_value, w_gate, w_out, mon_right, mon_left, twiddle, cotangent):
    seq_size, chan_size, dp_size = sizes
    _, length, width = inputs.shape
    size = mon_right.shape[0]
    blocks = length // size
    places = size // seq_size
    x, ct = inputs[0], cotangent[0]
    cols = places * width
    square = 2 * length * width * width

    cube = shape(length, width)
    weights = [pltpu.VMEM((width, width), BF16)] * 3
    tables = weights + [pltpu.VMEM((size, size), BF16), pltpu.VMEM((blocks, size), F32)]
    activations = pltpu.VMEM((length, width), BF16)
    exchanged = pltpu.VMEM((seq_size * blocks, 2 * cols), BF16)
    small = (w_value[0], w_gate[0], w_out[0], mon_right, twiddle)
    send = pl.pallas_call(
        functools.partial(rows_before, seq_size),
        out_shape=shape(seq_size * blocks, 2 * cols),
        in_specs=[HBM] * 7,
        out_specs=HBM,
        scratch_shapes=[
            activations, activations, *tables, exchanged,
            pltpu.VMEM((size, LANES), F32),
            exchanged,
            pltpu.SemaphoreType.DMA((5,)),
            pltpu.SemaphoreType.DMA((2, 4)),
            pltpu.SemaphoreType.DMA((8,)),
        ],
        compiler_params=params(60),
        cost_estimate=cost(4 * square, 8 * length * width),
        name="rows_before",
    )(x, ct, *small)
    came = lax.all_to_all(send, "seq", 0, 0, tiled=True)
    send_back, left_part = pl.pallas_call(
        columns,
        out_shape=(shape(seq_size * blocks, 2 * cols), shape(size, size, dtype=F32)),
        in_specs=[VMEM] * 2,
        out_specs=(VMEM,) * 2,
        compiler_params=params(20),
        cost_estimate=cost(3 * square, 8 * length * width),
        name="columns",
    )(mon_left, came)
    came_back = lax.all_to_all(send_back, "seq", 0, 0, tiled=True)
    half = shape(2 * size, 3 * LANES)
    grad_inputs, keep, give = pl.pallas_call(
        functools.partial(rows_after, seq_size),
        out_shape=(shape(length, width), half, half),
        in_specs=[HBM] * 9,
        out_specs=(HBM,) * 3,
        scratch_shapes=[
            activations,
            pltpu.VMEM(half.shape, BF16),
            pltpu.VMEM(half.shape, BF16),
            exchanged, activations, activations, *tables,
            pltpu.VMEM((size, size), F32),
            pltpu.VMEM((size, LANES), F32),
            exchanged, activations, activations, activations,
            pltpu.SemaphoreType.DMA((8,)),
            pltpu.SemaphoreType.DMA((6,)),
            pltpu.SemaphoreType.DMA((2, 4)),
            pltpu.SemaphoreType.DMA((4,)),
            pltpu.SemaphoreType.DMA((2,)),
        ],
        compiler_params=params(60),
        cost_estimate=cost(11 * square, 12 * length * width),
        name="rows_after",
    )(came_back, x, ct, *small, left_part)

    even = lax.axis_index("seq") % 2 == 0
    swap = [(i, i ^ 1) for i in range(seq_size)]
    like = [
        [seq * dp_size + dp for seq in range(core, seq_size, 2) for dp in range(dp_size)]
        for core in range(2)
    ]
    peers = len(like[0])
    theirs = lax.ppermute(give, "seq", swap)
    pair = (keep.astype(F32) + theirs.astype(F32)).astype(BF16)
    arrived = lax.all_to_all(pair, ("seq", "dp"), 0, 0, tiled=True, axis_index_groups=like)
    mine = jnp.sum(arrived.reshape(peers, -1, 3 * LANES).astype(F32), axis=0)
    factors = mine[None, :, LANES:].astype(BF16)
    factors = jnp.broadcast_to(factors, (chan_size,) + factors.shape[1:])
    factors = lax.all_to_all(factors, "chan", 0, 0, tiled=True).astype(F32)
    factors = jnp.sum(factors, axis=0)
    middle = jnp.where(even, mine[:, LANES : 2 * LANES], factors[:, :LANES])
    done = jnp.concatenate([mine[:, :LANES], middle, factors[:, LANES:]], axis=1).astype(BF16)
    spread = jnp.broadcast_to(done[None], (peers,) + done.shape).reshape(pair.shape)
    half = lax.all_to_all(spread, ("seq", "dp"), 0, 0, tiled=True, axis_index_groups=like)
    other = lax.ppermute(half, "seq", swap)
    g_value, g_gate, g_out, g_right, g_left, g_twiddle = pl.pallas_call(
        unpack,
        out_shape=(shape(size, size, dtype=F32),) * 5 + (shape(blocks, size, dtype=F32),),
        in_specs=[VMEM] * 2,
        out_specs=(VMEM,) * 6,
        compiler_params=params(20),
        name="unpack",
    )(half, other)
    return grad_inputs[None], g_value[None], g_gate[None], g_out[None], g_right, g_left, g_twiddle


def solution(mesh):
    sizes = tuple(mesh.shape[name] for name in ("seq", "chan", "dp"))
    return jax.shard_map(
        functools.partial(on_device, sizes),
        mesh=mesh,
        in_specs=(
            P("dp", "seq", "chan"),
            P("chan", None, None),
            P("chan", None, None),
            P("chan", None, None),
            P(),
            P(),
            P("seq", None),
            P("dp", "seq", "chan"),
        ),
        out_specs=(
            P("dp", "seq", "chan"),
            P("chan", None, None),
            P("chan", None, None),
            P("chan", None, None),
            P(),
            P(),
            P("seq", None),
        ),
        check_vma=False,
    )
```

```python
import functools

import jax
import jax.numpy as jnp
from jax import lax
from jax.experimental import pallas as pl
from jax.experimental.pallas import tpu as pltpu
from jax.sharding import PartitionSpec as P

F32 = jnp.float32
BF16 = jnp.bfloat16
LANES = 128
VMEM = pl.BlockSpec(memory_space=pltpu.VMEM)
HBM = pl.BlockSpec(memory_space=pl.ANY)


def params(mib):
    return pltpu.CompilerParams(vmem_limit_bytes=mib * 1024 * 1024)


def dot(a, b, dims=((1,), (0,))):
    return lax.dot_general(a, b, (dims, ((), ())), preferred_element_type=F32)


NT = ((1,), (1,))
TN = ((0,), (0,))


def every(ref, start, count, step):
    return ref[pl.ds(start, count, stride=step), :]


def place_major(ref, groups, places):
    return jnp.concatenate([every(ref, p, groups, places) for p in range(places)], axis=0)


def group_major(ref, value, groups, places):
    for p in range(places):
        ref[pl.ds(p, groups, stride=places), :] = value[p * groups : (p + 1) * groups]
    return ref[...]


def shuffle(outer, inner):
    size = outer * inner
    row = lax.broadcasted_iota(jnp.int32, (size, size), 0)
    column = lax.broadcasted_iota(jnp.int32, (size, size), 1)
    return jnp.where(column == (row % inner) * outer + row // inner, 1.0, 0.0).astype(BF16)


def rows_before(
    groups, x_hbm, ct_hbm, wv_hbm, wg_hbm, wo_hbm, right_hbm, twiddle_hbm,
    send_hbm, value_hbm, gate_hbm, back_hbm,
    x_ref, ct_ref, wv_ref, wg_ref, wo_ref, right_ref, twiddle_ref,
    send_ref, value_ref, gate_ref, back_ref, wide, cols, small_sems, in_sems, out_sems, send_sems,
):
    blocks = twiddle_ref.shape[0]
    size = right_ref.shape[0]
    places = size // groups
    width = x_ref.shape[1]
    parts = in_sems.shape[1]
    step = x_ref.shape[0] // parts
    small = [
        pltpu.make_async_copy(source, target, small_sems.at[n])
        for n, (source, target) in enumerate(
            (
                (wg_hbm, wg_ref), (wo_hbm, wo_ref), (wv_hbm, wv_ref),
                (right_hbm, right_ref), (twiddle_hbm, twiddle_ref),
            )
        )
    ]
    for copy in small:
        copy.start()
    copies = []
    for n in range(parts):
        rows = pl.ds(n * step, step)
        copies.append(
            (
                pltpu.make_async_copy(x_hbm.at[rows], x_ref.at[rows], in_sems.at[0, n]),
                pltpu.make_async_copy(ct_hbm.at[rows], ct_ref.at[rows], in_sems.at[1, n]),
            )
        )
        for copy in copies[-1]:
            copy.start()
    to_places = shuffle(places, groups)
    for copy in small:
        copy.wait()
    right = dot(to_places, right_ref[...]).astype(BF16)
    wide[...] = jnp.concatenate(
        [twiddle_ref[...], jnp.zeros((LANES - blocks, size), F32)], axis=0
    ).T
    twist = place_major(wide, groups, places)
    out = []
    for i in range(blocks):
        rows = slice(i * size, (i + 1) * size)
        if i * size % step == 0:
            for copy in copies[i * size // step]:
                copy.wait()
        x = x_ref[rows, :]
        gates = dot(x, wg_ref[...]).astype(BF16)
        back = dot(ct_ref[rows, :], wo_ref[...], NT).astype(BF16)
        values = dot(x, wv_ref[...]).astype(BF16)
        gate_ref[rows, :] = gates
        back_ref[rows, :] = back
        value_ref[rows, :] = values
        if (i + 1) * size % step == 0:
            n = i * size // step
            done = pl.ds(n * step, step)
            for k, (source, target) in enumerate(
                ((gate_ref, gate_hbm), (back_ref, back_hbm), (value_ref, value_hbm))
            ):
                out.append(
                    pltpu.make_async_copy(source.at[done], target.at[done], out_sems.at[k, n])
                )
                out[-1].start()
        mixed = (back.astype(F32) * gates.astype(F32)).astype(BF16)
        mixed = dot(to_places, mixed).astype(BF16)
        twisted = (dot(right, values) * twist[:, i : i + 1]).astype(BF16)
        for p in range(places):
            part = slice(p * groups, (p + 1) * groups)
            here = slice(i * groups, (i + 1) * groups)
            cols[here, p * width : (p + 1) * width] = mixed[part]
            cols[here, (places + p) * width : (places + p + 1) * width] = twisted[part]
    to_send = shuffle(groups, blocks)
    lanes = cols.shape[1] // send_sems.shape[0]
    for n in range(send_sems.shape[0]):
        at = slice(n * lanes, (n + 1) * lanes)
        send_ref[:, at] = dot(to_send, cols[:, at]).astype(BF16)
        part = pl.ds(n * lanes, lanes)
        out.append(
            pltpu.make_async_copy(send_ref.at[:, part], send_hbm.at[:, part], send_sems.at[n])
        )
        out[-1].start()
    for copy in out:
        copy.wait()


def columns(left_ref, cols_ref, send_ref, grad_ref):
    left = left_ref[...]
    half = cols_ref.shape[1] // 2
    for at in range(0, half, 512):
        back = cols_ref[:, at : at + 512]
        twist = cols_ref[:, half + at : half + at + 512]
        send_ref[:, at : at + 512] = dot(left, back, TN).astype(BF16)
        send_ref[:, half + at : half + at + 512] = dot(left, twist).astype(BF16)
    grad_ref[...] = dot(cols_ref[:, :half], cols_ref[:, half:], NT)


def input_grad(back_value_ref, back_gate_ref, wv_ref, wg_ref, gi_ref):
    for at in range(0, gi_ref.shape[0], 256):
        rows = slice(at, at + 256)
        gi_ref[rows, :] = (
            dot(back_value_ref[rows, :], wv_ref[...], NT)
            + dot(back_gate_ref[rows, :], wg_ref[...], NT)
        ).astype(BF16)


def rows_after(
    groups, came_ref, x_ref, ct_ref, value_ref, gate_ref, back_ref, right_ref, twiddle_ref,
    left_grad_ref,
    back_value_ref, back_gate_ref, keep_ref, give_ref,
    low_ref, high_ref, wide, cols, gated_all, rotated_all, turned_all,
):
    size = right_ref.shape[0]
    blocks = twiddle_ref.shape[0]
    places = size // groups
    width = x_ref.shape[1]
    to_blocks = shuffle(blocks, groups)
    to_groups = shuffle(groups, places)
    right = dot(shuffle(places, groups), right_ref[...]).astype(BF16)
    right_turned = right.T
    wide[...] = jnp.concatenate(
        [twiddle_ref[...], jnp.zeros((LANES - blocks, size), F32)], axis=0
    ).T
    twist = place_major(wide, groups, places)
    for at in range(0, cols.shape[1], 512):
        cols[:, at : at + 512] = dot(to_blocks, came_ref[:, at : at + 512]).astype(BF16)
    lane = lax.broadcasted_iota(jnp.int32, (size, LANES), 1)
    twist_grad = jnp.zeros((size, LANES), F32)
    for i in range(blocks):
        rows = slice(i * size, (i + 1) * size)
        here = slice(i * groups, (i + 1) * groups)
        values = value_ref[rows, :]
        turned_all[rows, :] = values.T
        back, mixed = (
            jnp.concatenate(
                [
                    cols[here, (first + p) * width : (first + p + 1) * width]
                    for p in range(places)
                ],
                axis=0,
            )
            for first in (0, places)
        )
        back = back.astype(F32)
        column = jnp.sum(back * dot(right, values), axis=1, keepdims=True)
        twist_grad = jnp.where(lane == i, column, twist_grad)
        back_rotated = (back * twist[:, i : i + 1]).astype(BF16)
        rotated_all[:, rows] = back_rotated
        back_value_ref[rows, :] = dot(right_turned, back_rotated).astype(BF16)
        mixed = dot(to_groups, mixed)
        back_gate_ref[rows, :] = (back_ref[rows, :].astype(F32) * mixed).astype(BF16)
        gated_all[rows, :] = (gate_ref[rows, :].astype(F32) * mixed).astype(BF16)

    def put(ref, tile, grad):
        for h in range(2):
            ref[h * size : (h + 1) * size, tile * LANES : (tile + 1) * LANES] = grad[
                :, h * LANES : (h + 1) * LANES
            ].astype(BF16)

    put(low_ref, 0, dot(x_ref[...], back_value_ref[...], TN))
    put(high_ref, 0, dot(x_ref[...], back_gate_ref[...], TN))
    put(low_ref, 1, dot(gated_all[...], ct_ref[...], TN))
    put(high_ref, 2, left_grad_ref[...])
    right_grad = dot(rotated_all[...], turned_all[...])
    for h in range(2):
        half = group_major(wide, right_grad[:, h * LANES : (h + 1) * LANES], groups, places)
        low_ref[h * size : (h + 1) * size, 2 * LANES :] = half.astype(BF16)
    flat = group_major(wide, twist_grad, groups, places).T[:blocks]
    own = jnp.concatenate([flat[:, :LANES], flat[:, LANES:]], axis=0).astype(BF16)
    high_ref[:, LANES : 2 * LANES] = jnp.zeros((2 * size, LANES), BF16)
    at = pl.multiple_of(lax.axis_index("seq") * 2 * blocks, 2 * blocks)
    high_ref[pl.ds(at, 2 * blocks), LANES : 2 * LANES] = own

    even = lax.axis_index("seq") % 2 == 0

    @pl.when(even)
    def _():
        keep_ref[...] = low_ref[...]
        give_ref[...] = high_ref[...]

    @pl.when(jnp.logical_not(even))
    def _():
        keep_ref[...] = high_ref[...]
        give_ref[...] = low_ref[...]


def sum_peers(came_ref, mine_ref, factors_ref):
    rows, lanes = mine_ref.shape
    total = jnp.sum(came_ref[...].astype(F32).reshape(-1, rows, lanes), axis=0)
    mine_ref[...] = total
    copies = factors_ref.shape[0] // rows
    factors_ref[...] = jnp.concatenate([total[:, LANES:]] * copies, axis=0).astype(BF16)


def sum_factors(mine_ref, came_ref, done_ref):
    rows, lanes = mine_ref.shape
    total = jnp.sum(came_ref[...].astype(F32).reshape(-1, rows, lanes - LANES), axis=0)
    even = lax.axis_index("seq") % 2 == 0
    middle = jnp.where(even, mine_ref[:, LANES : 2 * LANES], total[:, :LANES])
    done = jnp.concatenate([mine_ref[:, :LANES], middle, total[:, LANES:]], axis=1)
    pair = jnp.concatenate([done, done], axis=0).astype(BF16)
    for at in range(0, done_ref.shape[0], 2 * rows):
        done_ref[at : at + 2 * rows, :] = pair


def unpack(mine_ref, other_ref, value_ref, gate_ref, out_ref, right_ref, left_ref, twiddle_ref):
    size = value_ref.shape[0]
    blocks = twiddle_ref.shape[0]
    seq = lax.axis_index("seq")

    def take(ref, source, tile):
        for h in range(2):
            ref[:, h * LANES : (h + 1) * LANES] = source[
                h * size : (h + 1) * size, tile * LANES : (tile + 1) * LANES
            ].astype(F32)

    def spread(low, high):
        take(value_ref, low, 0)
        take(out_ref, low, 1)
        take(right_ref, low, 2)
        take(gate_ref, high, 0)
        take(left_ref, high, 2)
        at = pl.multiple_of(seq * 2 * blocks, 2 * blocks)
        own = high[pl.ds(at, 2 * blocks), LANES : 2 * LANES].astype(F32)
        twiddle_ref[:, :LANES] = own[:blocks]
        twiddle_ref[:, LANES:] = own[blocks:]

    @pl.when(seq % 2 == 0)
    def _():
        spread(mine_ref, other_ref)

    @pl.when(seq % 2 == 1)
    def _():
        spread(other_ref, mine_ref)


def shape(*dims, dtype=BF16):
    return jax.ShapeDtypeStruct(dims, dtype)


def cost(flops, moved):
    return pl.CostEstimate(flops=int(flops), bytes_accessed=int(moved), transcendentals=0)


def on_device(sizes, inputs, w_value, w_gate, w_out, mon_right, mon_left, twiddle, cotangent):
    seq_size, chan_size, dp_size = sizes
    _, length, width = inputs.shape
    size = mon_right.shape[0]
    blocks = length // size
    places = size // seq_size
    x, ct = inputs[0], cotangent[0]
    cols = places * width
    square = 2 * length * width * width

    cube = shape(length, width)
    weights = [pltpu.VMEM((width, width), BF16)] * 3
    tables = weights + [pltpu.VMEM((size, size), BF16), pltpu.VMEM((blocks, size), F32)]
    activations = pltpu.VMEM((length, width), BF16)
    exchanged = pltpu.VMEM((seq_size * blocks, 2 * cols), BF16)
    small = (w_value[0], w_gate[0], w_out[0], mon_right, twiddle)
    cube = shape(length, width)
    send, values, gates, back_gated = pl.pallas_call(
        functools.partial(rows_before, seq_size),
        out_shape=(shape(seq_size * blocks, 2 * cols), cube, cube, cube),
        in_specs=[HBM] * 7,
        out_specs=(HBM,) * 4,
        scratch_shapes=[
            activations, activations, *tables, exchanged, activations, activations, activations,
            pltpu.VMEM((size, LANES), F32),
            exchanged,
            pltpu.SemaphoreType.DMA((5,)),
            pltpu.SemaphoreType.DMA((2, 4)),
            pltpu.SemaphoreType.DMA((3, 4)),
            pltpu.SemaphoreType.DMA((8,)),
        ],
        compiler_params=params(60),
        cost_estimate=cost(4 * square, 14 * length * width),
        name="rows_before",
    )(x, ct, *small)
    came = lax.all_to_all(send, "seq", 0, 0, tiled=True)
    send_back, left_part = pl.pallas_call(
        columns,
        out_shape=(shape(seq_size * blocks, 2 * cols), shape(size, size, dtype=F32)),
        in_specs=[VMEM] * 2,
        out_specs=(VMEM,) * 2,
        compiler_params=params(20),
        cost_estimate=cost(3 * square, 8 * length * width),
        name="columns",
    )(mon_left, came)
    came_back = lax.all_to_all(send_back, "seq", 0, 0, tiled=True)
    half = shape(2 * size, 3 * LANES)
    back_values, back_gates, keep, give = pl.pallas_call(
        functools.partial(rows_after, seq_size),
        out_shape=(cube, cube, half, half),
        in_specs=[VMEM] * 9,
        out_specs=(VMEM,) * 4,
        scratch_shapes=[
            pltpu.VMEM(half.shape, BF16),
            pltpu.VMEM(half.shape, BF16),
            pltpu.VMEM((size, LANES), F32),
            exchanged,
            activations,
            pltpu.VMEM((size, length), BF16),
            activations,
        ],
        compiler_params=params(24),
        cost_estimate=cost(6 * square, 16 * length * width),
        name="rows_after",
    )(came_back, x, ct, values, gates, back_gated, mon_right, twiddle, left_part)
    grad_inputs = pl.pallas_call(
        input_grad,
        out_shape=cube,
        in_specs=[VMEM] * 4,
        out_specs=VMEM,
        compiler_params=params(20),
        cost_estimate=cost(2 * square, 6 * length * width),
        name="input_grad",
    )(back_values, back_gates, w_value[0], w_gate[0])

    swap = [(i, i ^ 1) for i in range(seq_size)]
    like = [
        [seq * dp_size + dp for seq in range(core, seq_size, 2) for dp in range(dp_size)]
        for core in range(2)
    ]
    peers = len(like[0])
    theirs = lax.ppermute(give, "seq", swap)
    pair = (keep.astype(F32) + theirs.astype(F32)).astype(BF16)
    arrived = lax.all_to_all(pair, ("seq", "dp"), 0, 0, tiled=True, axis_index_groups=like)
    rows = arrived.shape[0] // peers
    mine, factors = pl.pallas_call(
        sum_peers,
        out_shape=(
            shape(rows, 3 * LANES, dtype=F32),
            shape(chan_size * rows, 2 * LANES),
        ),
        in_specs=[VMEM],
        out_specs=(VMEM,) * 2,
        compiler_params=params(8),
        name="sum_peers",
    )(arrived)
    factors = lax.all_to_all(factors, "chan", 0, 0, tiled=True)
    spread = pl.pallas_call(
        sum_factors,
        out_shape=shape(*pair.shape),
        in_specs=[VMEM] * 2,
        out_specs=VMEM,
        compiler_params=params(8),
        name="sum_factors",
    )(mine, factors)
    half = lax.all_to_all(spread, ("seq", "dp"), 0, 0, tiled=True, axis_index_groups=like)
    other = lax.ppermute(half, "seq", swap)
    g_value, g_gate, g_out, g_right, g_left, g_twiddle = pl.pallas_call(
        unpack,
        out_shape=(shape(size, size, dtype=F32),) * 5 + (shape(blocks, size, dtype=F32),),
        in_specs=[VMEM] * 2,
        out_specs=(VMEM,) * 6,
        compiler_params=params(8),
        name="unpack",
    )(half, other)
    return grad_inputs[None], g_value[None], g_gate[None], g_out[None], g_right, g_left, g_twiddle


def solution(mesh):
    sizes = tuple(mesh.shape[name] for name in ("seq", "chan", "dp"))
    return jax.shard_map(
        functools.partial(on_device, sizes),
        mesh=mesh,
        in_specs=(
            P("dp", "seq", "chan"),
            P("chan", None, None),
            P("chan", None, None),
            P("chan", None, None),
            P(),
            P(),
            P("seq", None),
            P("dp", "seq", "chan"),
        ),
        out_specs=(
            P("dp", "seq", "chan"),
            P("chan", None, None),
            P("chan", None, None),
            P("chan", None, None),
            P(),
            P(),
            P("seq", None),
        ),
        check_vma=False,
    )
```

```python
import functools

import jax
import jax.numpy as jnp
from jax import lax
from jax.experimental import pallas as pl
from jax.experimental.pallas import tpu as pltpu
from jax.sharding import PartitionSpec as P

F32 = jnp.float32
BF16 = jnp.bfloat16
LANES = 128
VMEM = pl.BlockSpec(memory_space=pltpu.VMEM)
HBM = pl.BlockSpec(memory_space=pl.ANY)


def params(mib):
    return pltpu.CompilerParams(vmem_limit_bytes=mib * 1024 * 1024)


def dot(a, b, dims=((1,), (0,))):
    return lax.dot_general(a, b, (dims, ((), ())), preferred_element_type=F32)


NT = ((1,), (1,))
TN = ((0,), (0,))


def turned_twiddle(twiddle_ref):
    blocks, size = twiddle_ref.shape
    return jnp.concatenate([twiddle_ref[...], jnp.zeros((LANES - blocks, size), F32)], axis=0).T


def shuffle(outer, inner):
    size = outer * inner
    row = lax.broadcasted_iota(jnp.int32, (size, size), 0)
    column = lax.broadcasted_iota(jnp.int32, (size, size), 1)
    return jnp.where(column == (row % inner) * outer + row // inner, 1.0, 0.0).astype(BF16)


def rows_before(
    x_hbm, ct_hbm, wv_hbm, wg_hbm, wo_hbm, right_hbm, twiddle_hbm,
    send_hbm, value_hbm, gate_hbm, back_hbm,
    x_ref, ct_ref, wv_ref, wg_ref, wo_ref, right_ref, twiddle_ref,
    send_ref, value_ref, gate_ref, back_ref, small_sems, in_sems, out_sems, send_sems,
):
    blocks = twiddle_ref.shape[0]
    size = right_ref.shape[0]
    width = x_ref.shape[1]
    parts = in_sems.shape[1]
    step = x_ref.shape[0] // parts
    small = [
        pltpu.make_async_copy(source, target, small_sems.at[n])
        for n, (source, target) in enumerate(
            (
                (wg_hbm, wg_ref), (wo_hbm, wo_ref), (wv_hbm, wv_ref),
                (right_hbm, right_ref), (twiddle_hbm, twiddle_ref),
            )
        )
    ]
    for copy in small:
        copy.start()
    copies = []
    for n in range(parts):
        rows = pl.ds(n * step, step)
        copies.append(
            (
                pltpu.make_async_copy(x_hbm.at[rows], x_ref.at[rows], in_sems.at[0, n]),
                pltpu.make_async_copy(ct_hbm.at[rows], ct_ref.at[rows], in_sems.at[1, n]),
            )
        )
        for copy in copies[-1]:
            copy.start()
    for copy in small:
        copy.wait()
    right = right_ref[...]
    twist = turned_twiddle(twiddle_ref)
    out = []
    for i in range(blocks):
        rows = slice(i * size, (i + 1) * size)
        if i * size % step == 0:
            for copy in copies[i * size // step]:
                copy.wait()
        x = x_ref[rows, :]
        gates = dot(x, wg_ref[...]).astype(BF16)
        back = dot(ct_ref[rows, :], wo_ref[...], NT).astype(BF16)
        values = dot(x, wv_ref[...]).astype(BF16)
        gate_ref[rows, :] = gates
        back_ref[rows, :] = back
        value_ref[rows, :] = values
        if (i + 1) * size % step == 0:
            n = i * size // step
            done = pl.ds(n * step, step)
            for k, (source, target) in enumerate(
                ((gate_ref, gate_hbm), (back_ref, back_hbm), (value_ref, value_hbm))
            ):
                out.append(
                    pltpu.make_async_copy(source.at[done], target.at[done], out_sems.at[k, n])
                )
                out[-1].start()
        mixed = (back.astype(F32) * gates.astype(F32)).astype(BF16)
        twisted = (dot(right, values) * twist[:, i : i + 1]).astype(BF16)
        for k, part in enumerate((mixed, twisted)):
            at = (k * blocks + i) * width
            send_ref[:, at : at + width] = part
            lanes = pl.ds(at, width)
            out.append(
                pltpu.make_async_copy(
                    send_ref.at[:, lanes], send_hbm.at[:, lanes], send_sems.at[k, i]
                )
            )
            out[-1].start()
    for copy in out:
        copy.wait()


def columns(
    groups, blocks, left_ref, came_ref, send_ref, grad_ref, cols, mixed_cols, back_all, twist_all
):
    size = came_ref.shape[0]
    places = size // groups
    width = came_ref.shape[1] // (2 * blocks)
    to_places = shuffle(places, groups)
    to_groups = shuffle(groups, places)
    order = shuffle(blocks, groups)
    left = dot(order, left_ref[...]).astype(BF16)
    left = dot(left, order, NT).astype(BF16)
    for at in range(0, cols.shape[1], 512):
        cols[:, at : at + 512] = dot(to_places, came_ref[:, at : at + 512]).astype(BF16)
    for p in range(places):
        here = slice(p * groups, (p + 1) * groups)
        back, twist = (
            jnp.concatenate(
                [cols[here, (first + i) * width : (first + i + 1) * width] for i in range(blocks)],
                axis=0,
            )
            for first in (0, blocks)
        )
        back_all[:, p * width : (p + 1) * width] = back
        twist_all[:, p * width : (p + 1) * width] = twist
        mixed = (dot(left, back, TN).astype(BF16), dot(left, twist).astype(BF16))
        for k in range(2):
            for i in range(blocks):
                at = (k * blocks + i) * width
                mixed_cols[here, at : at + width] = mixed[k][i * groups : (i + 1) * groups]
    for at in range(0, cols.shape[1], 512):
        send_ref[:, at : at + 512] = dot(to_groups, mixed_cols[:, at : at + 512]).astype(BF16)
    grad = dot(back_all[...], twist_all[...], NT).astype(BF16)
    grad_ref[...] = dot(dot(order, grad, TN).astype(BF16), order)


def input_grad(back_value_ref, back_gate_ref, wv_ref, wg_ref, gi_ref):
    for at in range(0, gi_ref.shape[0], 256):
        rows = slice(at, at + 256)
        gi_ref[rows, :] = (
            dot(back_value_ref[rows, :], wv_ref[...], NT)
            + dot(back_gate_ref[rows, :], wg_ref[...], NT)
        ).astype(BF16)


def rows_after(
    came_ref, x_ref, ct_ref, value_ref, gate_ref, back_ref, right_ref, twiddle_ref,
    left_grad_ref,
    back_value_ref, back_gate_ref, keep_ref, give_ref,
    low_ref, high_ref, gated_all, rotated_all, turned_all,
):
    size = right_ref.shape[0]
    blocks = twiddle_ref.shape[0]
    width = x_ref.shape[1]
    right = right_ref[...]
    right_turned = right.T
    twist = turned_twiddle(twiddle_ref)
    lane = lax.broadcasted_iota(jnp.int32, (size, LANES), 1)
    twist_grad = jnp.zeros((size, LANES), F32)
    for i in range(blocks):
        rows = slice(i * size, (i + 1) * size)
        values = value_ref[rows, :]
        turned_all[rows, :] = values.T
        back = came_ref[:, i * width : (i + 1) * width].astype(F32)
        mixed = came_ref[:, (blocks + i) * width : (blocks + i + 1) * width].astype(F32)
        column = jnp.sum(back * dot(right, values), axis=1, keepdims=True)
        twist_grad = jnp.where(lane == i, column, twist_grad)
        back_rotated = (back * twist[:, i : i + 1]).astype(BF16)
        rotated_all[:, rows] = back_rotated
        back_value_ref[rows, :] = dot(right_turned, back_rotated).astype(BF16)
        back_gate_ref[rows, :] = (back_ref[rows, :].astype(F32) * mixed).astype(BF16)
        gated_all[rows, :] = (gate_ref[rows, :].astype(F32) * mixed).astype(BF16)

    def put(ref, tile, grad):
        for h in range(2):
            ref[h * size : (h + 1) * size, tile * LANES : (tile + 1) * LANES] = grad[
                :, h * LANES : (h + 1) * LANES
            ].astype(BF16)

    put(low_ref, 0, dot(x_ref[...], back_value_ref[...], TN))
    put(high_ref, 0, dot(x_ref[...], back_gate_ref[...], TN))
    put(low_ref, 1, dot(gated_all[...], ct_ref[...], TN))
    put(high_ref, 2, left_grad_ref[...])
    put(low_ref, 2, dot(rotated_all[...], turned_all[...]))
    flat = twist_grad.T[:blocks]
    own = jnp.concatenate([flat[:, :LANES], flat[:, LANES:]], axis=0).astype(BF16)
    high_ref[:, LANES : 2 * LANES] = jnp.zeros((2 * size, LANES), BF16)
    at = pl.multiple_of(lax.axis_index("seq") * 2 * blocks, 2 * blocks)
    high_ref[pl.ds(at, 2 * blocks), LANES : 2 * LANES] = own

    even = lax.axis_index("seq") % 2 == 0

    @pl.when(even)
    def _():
        keep_ref[...] = low_ref[...]
        give_ref[...] = high_ref[...]

    @pl.when(jnp.logical_not(even))
    def _():
        keep_ref[...] = high_ref[...]
        give_ref[...] = low_ref[...]


def sum_peers(came_ref, mine_ref, factors_ref):
    rows, lanes = mine_ref.shape
    total = jnp.sum(came_ref[...].astype(F32).reshape(-1, rows, lanes), axis=0)
    mine_ref[...] = total
    copies = factors_ref.shape[0] // rows
    factors_ref[...] = jnp.concatenate([total[:, LANES:]] * copies, axis=0).astype(BF16)


def sum_factors(mine_ref, came_ref, done_ref):
    rows, lanes = mine_ref.shape
    total = jnp.sum(came_ref[...].astype(F32).reshape(-1, rows, lanes - LANES), axis=0)
    even = lax.axis_index("seq") % 2 == 0
    middle = jnp.where(even, mine_ref[:, LANES : 2 * LANES], total[:, :LANES])
    done = jnp.concatenate([mine_ref[:, :LANES], middle, total[:, LANES:]], axis=1)
    pair = jnp.concatenate([done, done], axis=0).astype(BF16)
    for at in range(0, done_ref.shape[0], 2 * rows):
        done_ref[at : at + 2 * rows, :] = pair


def unpack(mine_ref, other_ref, value_ref, gate_ref, out_ref, right_ref, left_ref, twiddle_ref):
    size = value_ref.shape[0]
    blocks = twiddle_ref.shape[0]
    seq = lax.axis_index("seq")

    def take(ref, source, tile):
        for h in range(2):
            ref[:, h * LANES : (h + 1) * LANES] = source[
                h * size : (h + 1) * size, tile * LANES : (tile + 1) * LANES
            ].astype(F32)

    def spread(low, high):
        take(value_ref, low, 0)
        take(out_ref, low, 1)
        take(right_ref, low, 2)
        take(gate_ref, high, 0)
        take(left_ref, high, 2)
        at = pl.multiple_of(seq * 2 * blocks, 2 * blocks)
        own = high[pl.ds(at, 2 * blocks), LANES : 2 * LANES].astype(F32)
        twiddle_ref[:, :LANES] = own[:blocks]
        twiddle_ref[:, LANES:] = own[blocks:]

    @pl.when(seq % 2 == 0)
    def _():
        spread(mine_ref, other_ref)

    @pl.when(seq % 2 == 1)
    def _():
        spread(other_ref, mine_ref)


def shape(*dims, dtype=BF16):
    return jax.ShapeDtypeStruct(dims, dtype)


def cost(flops, moved):
    return pl.CostEstimate(flops=int(flops), bytes_accessed=int(moved), transcendentals=0)


def on_device(sizes, inputs, w_value, w_gate, w_out, mon_right, mon_left, twiddle, cotangent):
    seq_size, chan_size, dp_size = sizes
    _, length, width = inputs.shape
    size = mon_right.shape[0]
    blocks = length // size
    places = size // seq_size
    x, ct = inputs[0], cotangent[0]
    cols = places * width
    square = 2 * length * width * width

    cube = shape(length, width)
    weights = [pltpu.VMEM((width, width), BF16)] * 3
    tables = weights + [pltpu.VMEM((size, size), BF16), pltpu.VMEM((blocks, size), F32)]
    activations = pltpu.VMEM((length, width), BF16)
    exchanged = pltpu.VMEM((seq_size * blocks, 2 * cols), BF16)
    small = (w_value[0], w_gate[0], w_out[0], mon_right, twiddle)
    cube = shape(length, width)
    send, values, gates, back_gated = pl.pallas_call(
        rows_before,
        out_shape=(shape(seq_size * blocks, 2 * cols), cube, cube, cube),
        in_specs=[HBM] * 7,
        out_specs=(HBM,) * 4,
        scratch_shapes=[
            activations, activations, *tables, exchanged, activations, activations, activations,
            pltpu.SemaphoreType.DMA((5,)),
            pltpu.SemaphoreType.DMA((2, 4)),
            pltpu.SemaphoreType.DMA((3, 4)),
            pltpu.SemaphoreType.DMA((2, blocks)),
        ],
        compiler_params=params(60),
        cost_estimate=cost(4 * square, 14 * length * width),
        name="rows_before",
    )(x, ct, *small)
    came = lax.all_to_all(send, "seq", 0, 0, tiled=True)
    send_back, left_part = pl.pallas_call(
        functools.partial(columns, seq_size, blocks),
        out_shape=(shape(seq_size * blocks, 2 * cols), shape(size, size, dtype=F32)),
        in_specs=[VMEM] * 2,
        out_specs=(VMEM,) * 2,
        scratch_shapes=[
            exchanged,
            exchanged,
            pltpu.VMEM((seq_size * blocks, cols), BF16),
            pltpu.VMEM((seq_size * blocks, cols), BF16),
        ],
        compiler_params=params(24),
        cost_estimate=cost(3 * square, 8 * length * width),
        name="columns",
    )(mon_left, came)
    came_back = lax.all_to_all(send_back, "seq", 0, 0, tiled=True)
    half = shape(2 * size, 3 * LANES)
    back_values, back_gates, keep, give = pl.pallas_call(
        rows_after,
        out_shape=(cube, cube, half, half),
        in_specs=[VMEM] * 9,
        out_specs=(VMEM,) * 4,
        scratch_shapes=[
            pltpu.VMEM(half.shape, BF16),
            pltpu.VMEM(half.shape, BF16),
            activations,
            pltpu.VMEM((size, length), BF16),
            activations,
        ],
        compiler_params=params(24),
        cost_estimate=cost(6 * square, 16 * length * width),
        name="rows_after",
    )(came_back, x, ct, values, gates, back_gated, mon_right, twiddle, left_part)
    grad_inputs = pl.pallas_call(
        input_grad,
        out_shape=cube,
        in_specs=[VMEM] * 4,
        out_specs=VMEM,
        compiler_params=params(20),
        cost_estimate=cost(2 * square, 6 * length * width),
        name="input_grad",
    )(back_values, back_gates, w_value[0], w_gate[0])

    swap = [(i, i ^ 1) for i in range(seq_size)]
    like = [
        [seq * dp_size + dp for seq in range(core, seq_size, 2) for dp in range(dp_size)]
        for core in range(2)
    ]
    peers = len(like[0])
    theirs = lax.ppermute(give, "seq", swap)
    pair = (keep.astype(F32) + theirs.astype(F32)).astype(BF16)
    arrived = lax.all_to_all(pair, ("seq", "dp"), 0, 0, tiled=True, axis_index_groups=like)
    rows = arrived.shape[0] // peers
    mine, factors = pl.pallas_call(
        sum_peers,
        out_shape=(
            shape(rows, 3 * LANES, dtype=F32),
            shape(chan_size * rows, 2 * LANES),
        ),
        in_specs=[VMEM],
        out_specs=(VMEM,) * 2,
        compiler_params=params(8),
        name="sum_peers",
    )(arrived)
    factors = lax.all_to_all(factors, "chan", 0, 0, tiled=True)
    spread = pl.pallas_call(
        sum_factors,
        out_shape=shape(*pair.shape),
        in_specs=[VMEM] * 2,
        out_specs=VMEM,
        compiler_params=params(8),
        name="sum_factors",
    )(mine, factors)
    half = lax.all_to_all(spread, ("seq", "dp"), 0, 0, tiled=True, axis_index_groups=like)
    other = lax.ppermute(half, "seq", swap)
    g_value, g_gate, g_out, g_right, g_left, g_twiddle = pl.pallas_call(
        unpack,
        out_shape=(shape(size, size, dtype=F32),) * 5 + (shape(blocks, size, dtype=F32),),
        in_specs=[VMEM] * 2,
        out_specs=(VMEM,) * 6,
        compiler_params=params(8),
        name="unpack",
    )(half, other)
    return grad_inputs[None], g_value[None], g_gate[None], g_out[None], g_right, g_left, g_twiddle


def solution(mesh):
    sizes = tuple(mesh.shape[name] for name in ("seq", "chan", "dp"))
    return jax.shard_map(
        functools.partial(on_device, sizes),
        mesh=mesh,
        in_specs=(
            P("dp", "seq", "chan"),
            P("chan", None, None),
            P("chan", None, None),
            P("chan", None, None),
            P(),
            P(),
            P("seq", None),
            P("dp", "seq", "chan"),
        ),
        out_specs=(
            P("dp", "seq", "chan"),
            P("chan", None, None),
            P("chan", None, None),
            P("chan", None, None),
            P(),
            P(),
            P("seq", None),
        ),
        check_vma=False,
    )
```

```python
import functools

import jax
import jax.numpy as jnp
from jax import lax
from jax.experimental import pallas as pl
from jax.experimental.pallas import tpu as pltpu
from jax.sharding import PartitionSpec as P

F32 = jnp.float32
BF16 = jnp.bfloat16
LANES = 128
VMEM = pl.BlockSpec(memory_space=pltpu.VMEM)
HBM = pl.BlockSpec(memory_space=pl.ANY)


def params(mib):
    return pltpu.CompilerParams(vmem_limit_bytes=mib * 1024 * 1024)


def dot(a, b, dims=((1,), (0,))):
    return lax.dot_general(a, b, (dims, ((), ())), preferred_element_type=F32)


NT = ((1,), (1,))
TN = ((0,), (0,))


def turned_twiddle(twiddle_ref):
    blocks, size = twiddle_ref.shape
    return jnp.concatenate([twiddle_ref[...], jnp.zeros((LANES - blocks, size), F32)], axis=0).T


def shuffle(outer, inner):
    size = outer * inner
    row = lax.broadcasted_iota(jnp.int32, (size, size), 0)
    column = lax.broadcasted_iota(jnp.int32, (size, size), 1)
    return jnp.where(column == (row % inner) * outer + row // inner, 1.0, 0.0).astype(BF16)


def rows_before(
    x_hbm, ct_hbm, wv_hbm, wg_hbm, wo_hbm, right_hbm, twiddle_hbm,
    send_hbm, value_hbm, gate_hbm, back_hbm,
    x_ref, ct_ref, wv_ref, wg_ref, wo_ref, right_ref, twiddle_ref,
    send_ref, value_ref, gate_ref, back_ref, small_sems, in_sems, out_sems, send_sems,
):
    blocks = twiddle_ref.shape[0]
    size = right_ref.shape[0]
    width = x_ref.shape[1]
    parts = in_sems.shape[1]
    step = x_ref.shape[0] // parts
    small = [
        pltpu.make_async_copy(source, target, small_sems.at[n])
        for n, (source, target) in enumerate(
            (
                (wg_hbm, wg_ref), (wo_hbm, wo_ref), (wv_hbm, wv_ref),
                (right_hbm, right_ref), (twiddle_hbm, twiddle_ref),
            )
        )
    ]
    for copy in small:
        copy.start()
    copies = []
    for n in range(parts):
        rows = pl.ds(n * step, step)
        copies.append(
            (
                pltpu.make_async_copy(x_hbm.at[rows], x_ref.at[rows], in_sems.at[0, n]),
                pltpu.make_async_copy(ct_hbm.at[rows], ct_ref.at[rows], in_sems.at[1, n]),
            )
        )
        for copy in copies[-1]:
            copy.start()
    for copy in small:
        copy.wait()
    right = right_ref[...]
    twist = turned_twiddle(twiddle_ref)
    out = []
    for i in range(blocks):
        rows = slice(i * size, (i + 1) * size)
        if i * size % step == 0:
            for copy in copies[i * size // step]:
                copy.wait()
        x = x_ref[rows, :]
        gates = dot(x, wg_ref[...]).astype(BF16)
        back = dot(ct_ref[rows, :], wo_ref[...], NT).astype(BF16)
        values = dot(x, wv_ref[...]).astype(BF16)
        gate_ref[rows, :] = gates
        back_ref[rows, :] = back
        value_ref[rows, :] = values
        if (i + 1) * size % step == 0:
            n = i * size // step
            done = pl.ds(n * step, step)
            for k, (source, target) in enumerate(
                ((gate_ref, gate_hbm), (back_ref, back_hbm), (value_ref, value_hbm))
            ):
                out.append(
                    pltpu.make_async_copy(source.at[done], target.at[done], out_sems.at[k, n])
                )
                out[-1].start()
        mixed = (back.astype(F32) * gates.astype(F32)).astype(BF16)
        twisted = (dot(right, values) * twist[:, i : i + 1]).astype(BF16)
        for k, part in enumerate((mixed, twisted)):
            at = (k * blocks + i) * width
            send_ref[:, at : at + width] = part
            lanes = pl.ds(at, width)
            out.append(
                pltpu.make_async_copy(
                    send_ref.at[:, lanes], send_hbm.at[:, lanes], send_sems.at[k, i]
                )
            )
            out[-1].start()
    for copy in out:
        copy.wait()


def columns(
    groups, blocks, left_ref, came_ref, send_ref, grad_ref, cols, mixed_cols, back_all, twist_all
):
    size = came_ref.shape[0]
    places = size // groups
    width = came_ref.shape[1] // (2 * blocks)
    to_places = shuffle(places, groups)
    to_groups = shuffle(groups, places)
    order = shuffle(blocks, groups)
    left = dot(order, left_ref[...]).astype(BF16)
    left = dot(left, order, NT).astype(BF16)
    for at in range(0, cols.shape[1], 512):
        cols[:, at : at + 512] = dot(to_places, came_ref[:, at : at + 512]).astype(BF16)
    for p in range(places):
        here = slice(p * groups, (p + 1) * groups)
        back, twist = (
            jnp.concatenate(
                [cols[here, (first + i) * width : (first + i + 1) * width] for i in range(blocks)],
                axis=0,
            )
            for first in (0, blocks)
        )
        back_all[:, p * width : (p + 1) * width] = back
        twist_all[:, p * width : (p + 1) * width] = twist
        mixed = (dot(left, back, TN).astype(BF16), dot(left, twist).astype(BF16))
        for k in range(2):
            for i in range(blocks):
                at = (k * blocks + i) * width
                mixed_cols[here, at : at + width] = mixed[k][i * groups : (i + 1) * groups]
    for at in range(0, cols.shape[1], 512):
        send_ref[:, at : at + 512] = dot(to_groups, mixed_cols[:, at : at + 512]).astype(BF16)
    grad = dot(back_all[...], twist_all[...], NT).astype(BF16)
    grad_ref[...] = dot(dot(order, grad, TN).astype(BF16), order)


def input_grad(back_value_ref, back_gate_ref, wv_ref, wg_ref, gi_ref):
    for at in range(0, gi_ref.shape[0], 256):
        rows = slice(at, at + 256)
        gi_ref[rows, :] = (
            dot(back_value_ref[rows, :], wv_ref[...], NT)
            + dot(back_gate_ref[rows, :], wg_ref[...], NT)
        ).astype(BF16)


def rows_after(
    came_ref, x_ref, ct_ref, value_ref, gate_ref, back_ref, right_ref, twiddle_ref,
    left_grad_ref,
    back_value_ref, back_gate_ref, keep_ref, give_ref,
    low_ref, high_ref, gated_all, rotated_all, turned_all,
):
    size = right_ref.shape[0]
    blocks = twiddle_ref.shape[0]
    width = x_ref.shape[1]
    right = right_ref[...]
    right_turned = right.T
    twist = turned_twiddle(twiddle_ref)
    lane = lax.broadcasted_iota(jnp.int32, (size, LANES), 1)
    twist_grad = jnp.zeros((size, LANES), F32)
    for i in range(blocks):
        rows = slice(i * size, (i + 1) * size)
        values = value_ref[rows, :]
        turned_all[rows, :] = values.T
        back = came_ref[:, i * width : (i + 1) * width].astype(F32)
        mixed = came_ref[:, (blocks + i) * width : (blocks + i + 1) * width].astype(F32)
        column = jnp.sum(back * dot(right, values), axis=1, keepdims=True)
        twist_grad = jnp.where(lane == i, column, twist_grad)
        back_rotated = (back * twist[:, i : i + 1]).astype(BF16)
        rotated_all[:, rows] = back_rotated
        back_value_ref[rows, :] = dot(right_turned, back_rotated).astype(BF16)
        back_gate_ref[rows, :] = (back_ref[rows, :].astype(F32) * mixed).astype(BF16)
        gated_all[rows, :] = (gate_ref[rows, :].astype(F32) * mixed).astype(BF16)

    def put(ref, tile, grad):
        for h in range(2):
            ref[h * size : (h + 1) * size, tile * LANES : (tile + 1) * LANES] = grad[
                :, h * LANES : (h + 1) * LANES
            ].astype(BF16)

    put(low_ref, 0, dot(x_ref[...], back_value_ref[...], TN))
    put(high_ref, 0, dot(x_ref[...], back_gate_ref[...], TN))
    put(low_ref, 1, dot(gated_all[...], ct_ref[...], TN))
    put(high_ref, 2, left_grad_ref[...])
    put(low_ref, 2, dot(rotated_all[...], turned_all[...]))
    flat = twist_grad.T[:blocks]
    own = jnp.concatenate([flat[:, :LANES], flat[:, LANES:]], axis=0).astype(BF16)
    high_ref[:, LANES : 2 * LANES] = jnp.zeros((2 * size, LANES), BF16)
    at = pl.multiple_of(lax.axis_index("seq") * 2 * blocks, 2 * blocks)
    high_ref[pl.ds(at, 2 * blocks), LANES : 2 * LANES] = own

    even = lax.axis_index("seq") % 2 == 0

    @pl.when(even)
    def _():
        keep_ref[...] = low_ref[...]
        give_ref[...] = high_ref[...]

    @pl.when(jnp.logical_not(even))
    def _():
        keep_ref[...] = high_ref[...]
        give_ref[...] = low_ref[...]


def sum_peers(came_ref, mine_ref, factors_ref):
    rows, lanes = mine_ref.shape
    total = jnp.sum(came_ref[...].astype(F32).reshape(-1, rows, lanes), axis=0)
    mine_ref[...] = total
    copies = factors_ref.shape[0] // rows
    factors_ref[...] = jnp.concatenate([total[:, LANES:]] * copies, axis=0).astype(BF16)


def sum_factors(mine_ref, came_ref, done_ref):
    rows, lanes = mine_ref.shape
    total = jnp.sum(came_ref[...].astype(F32).reshape(-1, rows, lanes - LANES), axis=0)
    even = lax.axis_index("seq") % 2 == 0
    middle = jnp.where(even, mine_ref[:, LANES : 2 * LANES], total[:, :LANES])
    done = jnp.concatenate([mine_ref[:, :LANES], middle, total[:, LANES:]], axis=1)
    pair = jnp.concatenate([done, done], axis=0).astype(BF16)
    for at in range(0, done_ref.shape[0], 2 * rows):
        done_ref[at : at + 2 * rows, :] = pair


def unpack(mine_ref, other_ref, value_ref, gate_ref, out_ref, right_ref, left_ref, twiddle_ref):
    size = value_ref.shape[0]
    blocks = twiddle_ref.shape[0]
    seq = lax.axis_index("seq")

    def take(ref, source, tile):
        for h in range(2):
            ref[:, h * LANES : (h + 1) * LANES] = source[
                h * size : (h + 1) * size, tile * LANES : (tile + 1) * LANES
            ].astype(F32)

    def spread(low, high):
        take(value_ref, low, 0)
        take(out_ref, low, 1)
        take(right_ref, low, 2)
        take(gate_ref, high, 0)
        take(left_ref, high, 2)
        at = pl.multiple_of(seq * 2 * blocks, 2 * blocks)
        own = high[pl.ds(at, 2 * blocks), LANES : 2 * LANES].astype(F32)
        twiddle_ref[:, :LANES] = own[:blocks]
        twiddle_ref[:, LANES:] = own[blocks:]

    @pl.when(seq % 2 == 0)
    def _():
        spread(mine_ref, other_ref)

    @pl.when(seq % 2 == 1)
    def _():
        spread(other_ref, mine_ref)


def shape(*dims, dtype=BF16):
    return jax.ShapeDtypeStruct(dims, dtype)


def cost(flops, moved):
    return pl.CostEstimate(flops=int(flops), bytes_accessed=int(moved), transcendentals=0)


def on_device(sizes, inputs, w_value, w_gate, w_out, mon_right, mon_left, twiddle, cotangent):
    seq_size, chan_size, dp_size = sizes
    _, length, width = inputs.shape
    size = mon_right.shape[0]
    blocks = length // size
    places = size // seq_size
    x, ct = inputs[0], cotangent[0]
    cols = places * width
    square = 2 * length * width * width

    cube = shape(length, width)
    weights = [pltpu.VMEM((width, width), BF16)] * 3
    tables = weights + [pltpu.VMEM((size, size), BF16), pltpu.VMEM((blocks, size), F32)]
    activations = pltpu.VMEM((length, width), BF16)
    exchanged = pltpu.VMEM((seq_size * blocks, 2 * cols), BF16)
    small = (w_value[0], w_gate[0], w_out[0], mon_right, twiddle)
    cube = shape(length, width)
    send, values, gates, back_gated = pl.pallas_call(
        rows_before,
        out_shape=(shape(seq_size * blocks, 2 * cols), cube, cube, cube),
        in_specs=[HBM] * 7,
        out_specs=(HBM,) * 4,
        scratch_shapes=[
            activations, activations, *tables, exchanged, activations, activations, activations,
            pltpu.SemaphoreType.DMA((5,)),
            pltpu.SemaphoreType.DMA((2, blocks)),
            pltpu.SemaphoreType.DMA((3, blocks)),
            pltpu.SemaphoreType.DMA((2, blocks)),
        ],
        compiler_params=params(60),
        cost_estimate=cost(4 * square, 14 * length * width),
        name="rows_before",
    )(x, ct, *small)
    came = lax.all_to_all(send, "seq", 0, 0, tiled=True)
    send_back, left_part = pl.pallas_call(
        functools.partial(columns, seq_size, blocks),
        out_shape=(shape(seq_size * blocks, 2 * cols), shape(size, size, dtype=F32)),
        in_specs=[VMEM] * 2,
        out_specs=(VMEM,) * 2,
        scratch_shapes=[
            exchanged,
            exchanged,
            pltpu.VMEM((seq_size * blocks, cols), BF16),
            pltpu.VMEM((seq_size * blocks, cols), BF16),
        ],
        compiler_params=params(24),
        cost_estimate=cost(3 * square, 8 * length * width),
        name="columns",
    )(mon_left, came)
    came_back = lax.all_to_all(send_back, "seq", 0, 0, tiled=True)
    half = shape(2 * size, 3 * LANES)
    back_values, back_gates, keep, give = pl.pallas_call(
        rows_after,
        out_shape=(cube, cube, half, half),
        in_specs=[VMEM] * 9,
        out_specs=(VMEM,) * 4,
        scratch_shapes=[
            pltpu.VMEM(half.shape, BF16),
            pltpu.VMEM(half.shape, BF16),
            activations,
            pltpu.VMEM((size, length), BF16),
            activations,
        ],
        compiler_params=params(24),
        cost_estimate=cost(6 * square, 16 * length * width),
        name="rows_after",
    )(came_back, x, ct, values, gates, back_gated, mon_right, twiddle, left_part)
    grad_inputs = pl.pallas_call(
        input_grad,
        out_shape=cube,
        in_specs=[VMEM] * 4,
        out_specs=VMEM,
        compiler_params=params(20),
        cost_estimate=cost(2 * square, 6 * length * width),
        name="input_grad",
    )(back_values, back_gates, w_value[0], w_gate[0])

    swap = [(i, i ^ 1) for i in range(seq_size)]
    like = [
        [seq * dp_size + dp for seq in range(core, seq_size, 2) for dp in range(dp_size)]
        for core in range(2)
    ]
    peers = len(like[0])
    theirs = lax.ppermute(give, "seq", swap)
    pair = (keep.astype(F32) + theirs.astype(F32)).astype(BF16)
    arrived = lax.all_to_all(pair, ("seq", "dp"), 0, 0, tiled=True, axis_index_groups=like)
    rows = arrived.shape[0] // peers
    mine, factors = pl.pallas_call(
        sum_peers,
        out_shape=(
            shape(rows, 3 * LANES, dtype=F32),
            shape(chan_size * rows, 2 * LANES),
        ),
        in_specs=[VMEM],
        out_specs=(VMEM,) * 2,
        compiler_params=params(8),
        name="sum_peers",
    )(arrived)
    factors = lax.all_to_all(factors, "chan", 0, 0, tiled=True)
    spread = pl.pallas_call(
        sum_factors,
        out_shape=shape(*pair.shape),
        in_specs=[VMEM] * 2,
        out_specs=VMEM,
        compiler_params=params(8),
        name="sum_factors",
    )(mine, factors)
    half = lax.all_to_all(spread, ("seq", "dp"), 0, 0, tiled=True, axis_index_groups=like)
    other = lax.ppermute(half, "seq", swap)
    g_value, g_gate, g_out, g_right, g_left, g_twiddle = pl.pallas_call(
        unpack,
        out_shape=(shape(size, size, dtype=F32),) * 5 + (shape(blocks, size, dtype=F32),),
        in_specs=[VMEM] * 2,
        out_specs=(VMEM,) * 6,
        compiler_params=params(8),
        name="unpack",
    )(half, other)
    return grad_inputs[None], g_value[None], g_gate[None], g_out[None], g_right, g_left, g_twiddle


def solution(mesh):
    sizes = tuple(mesh.shape[name] for name in ("seq", "chan", "dp"))
    return jax.shard_map(
        functools.partial(on_device, sizes),
        mesh=mesh,
        in_specs=(
            P("dp", "seq", "chan"),
            P("chan", None, None),
            P("chan", None, None),
            P("chan", None, None),
            P(),
            P(),
            P("seq", None),
            P("dp", "seq", "chan"),
        ),
        out_specs=(
            P("dp", "seq", "chan"),
            P("chan", None, None),
            P("chan", None, None),
            P("chan", None, None),
            P(),
            P(),
            P("seq", None),
        ),
        check_vma=False,
    )
```
